128 devices in a mesh: wide: 16 (over x, y_hi, core), narrow: 8 (over y_lo, z).
Axes of the slice: x: 4, y: 4 (y_hi: 2, y_lo: 2; y = y_hi * 2 + y_lo), z: 4, core: 2. Of those that a mesh axis runs over, the one named last changes fastest.
Arguments:
- voltages: bfloat16 [2048, 262144], P('wide', 'narrow'), as said below
Outputs:
- visibility: float32 [128, 2048, 2048], P(('wide', 'narrow'))
Inputs may be any that keep to these rules, and one draw needn't show every extreme that they name: Real voltages; the power of an input may vary over the window.
All inputs are finite; a program needn't handle non-finite values.
Results may differ from the reference program's by a relative error of at most 0.0013.
Values may be sent and summed in bfloat16 or wider, within the bound.
A program may use at most 128 MiB of HBM per device.

```python
import math
import jax
import jax.numpy as jnp
from jax import lax

S = 2048
L = 512
TAPS = 4
CHAN = 128
FRAMES = 512


def draw_voltages(key, part):
    key = jax.random.fold_in(key, 11)
    keys = jax.random.split(key, 5)
    samples = FRAMES * L
    moment = jnp.arange(samples, dtype=jnp.float32)
    envelope = 1.0 + 2.0 * moment / samples
    noise = jnp.clip(jax.random.normal(keys[0], (S, samples), jnp.float32), -4.0, 4.0)
    spread = math.log(10.0)
    common_weight = 0.5
    amplitude = jnp.exp(jax.random.uniform(keys[1], (S, 1), jnp.float32, 0.0, spread))
    sources = jnp.clip(jax.random.normal(keys[2], (2, samples + 64), jnp.float32), -4.0, 4.0)
    delays = jax.random.randint(keys[3], (S, 2), 0, 64)
    gains = jnp.clip(jax.random.normal(keys[4], (S, 2), jnp.float32), -2.0, 2.0)

    def delayed(delay_pair, gain_pair):
        first = lax.dynamic_slice_in_dim(sources[0], delay_pair[0], samples)
        second = lax.dynamic_slice_in_dim(sources[1], delay_pair[1], samples)
        return gain_pair[0] * first + gain_pair[1] * second
    common = jax.vmap(delayed)(delays, gains)
    signal = 0.8 * noise + common_weight * common
    return (amplitude * envelope[None, :] * signal).astype(jnp.bfloat16)


def setup_inputs(seed: int = 0) -> dict:
    seeds = jax.random.split(jax.random.key(seed), 2)
    voltages = draw_voltages(jax.random.fold_in(seeds[1], 71), 0)
    return dict(voltages=voltages)


def channel_table(count):
    index = jnp.arange(L, dtype=jnp.int32)[:, None]
    channel = jnp.arange(count, dtype=jnp.int32)[None, :]
    angle = (index * channel % L).astype(jnp.float32) * (2.0 * math.pi / L)
    return jnp.concatenate([jnp.cos(angle), -jnp.sin(angle)], axis=1).astype(jnp.bfloat16)

def taper_table():
    place = jnp.arange(TAPS * L, dtype=jnp.float32)
    offset = (place - TAPS * L / 2.0 + 0.5) / L
    window = 0.5 - 0.5 * jnp.cos(2.0 * math.pi * (place + 0.5) / (TAPS * L))
    return (jnp.sinc(offset) * window).reshape(TAPS, L)

def filter_frames(frames, taper):
    count = frames.shape[1] - TAPS + 1
    total = jnp.zeros((frames.shape[0], count, L), jnp.float32)
    for step in range(TAPS):
        total = total + frames[:, step:step + count, :].astype(jnp.float32) * taper[step]
    return total.astype(jnp.bfloat16)

def reference(voltages):
    table = channel_table(CHAN)
    taper = taper_table()
    block = min(128, S)
    padded = jnp.concatenate([jnp.zeros((S, (TAPS - 1) * L), jnp.bfloat16), voltages], axis=1)
    padded = padded.reshape(S // block, block, FRAMES + TAPS - 1, L)

    def channelize(frames):
        filtered = filter_frames(frames, taper)
        spectrum = jnp.dot(filtered.reshape(block * FRAMES, L), table, preferred_element_type=jnp.float32)
        spectrum = spectrum.reshape(block, FRAMES, 2 * CHAN)
        sums = lax.optimization_barrier(jnp.sum(spectrum * spectrum, axis=1))
        power = (sums[:, :CHAN] + sums[:, CHAN:]) / FRAMES
        factor = 1.0 / jnp.sqrt(power + 1e-06)
        factor = jnp.concatenate([factor, factor], axis=1)
        return (spectrum * factor[:, None, :]).astype(jnp.bfloat16)
    requantized = lax.map(channelize, padded).reshape(S, FRAMES, 2 * CHAN)
    ordered = jnp.transpose(requantized, (2, 0, 1))
    row = lax.broadcasted_iota(jnp.int32, (S, S), 0)
    col = lax.broadcasted_iota(jnp.int32, (S, S), 1)

    def correlate(channel):
        real_rows = lax.dynamic_index_in_dim(ordered, channel, 0, keepdims=False)
        imag_rows = lax.dynamic_index_in_dim(ordered, channel + CHAN, 0, keepdims=False)
        joined = jnp.concatenate([real_rows, imag_rows], axis=1)
        turned = jnp.concatenate([imag_rows, -real_rows], axis=1)
        real_part = jnp.dot(joined, joined.T, preferred_element_type=jnp.float32)
        imag_part = jnp.dot(turned, joined.T, preferred_element_type=jnp.float32)
        return jnp.where(row >= col, real_part, imag_part) / FRAMES
    return lax.map(correlate, jnp.arange(CHAN, dtype=jnp.int32))
```

```python
import functools
import math

import jax
import jax.numpy as jnp
from jax import lax
from jax.experimental import pallas as pl
from jax.experimental.pallas import tpu as pltpu
from jax.sharding import PartitionSpec as P

S = 2048
L = 512
TAPS = 4
CHAN = 128
FRAMES = 512
WIDE = 16
NARROW = 8
ROWS = S // WIDE
FR_DEV = FRAMES // NARROW
HIST = (TAPS - 1) * L
STEP = 16
CHUNKS = FR_DEV // STEP
ORDER = (1, 2, 3, 0)
KB = 2 * STEP * NARROW
TILE = 256
MESH = pl.DeviceIdType.MESH


def channel_table(count):
    index = jnp.arange(L, dtype=jnp.int32)[:, None]
    channel = jnp.arange(count, dtype=jnp.int32)[None, :]
    angle = (index * channel % L).astype(jnp.float32) * (2.0 * math.pi / L)
    return jnp.concatenate([jnp.cos(angle), -jnp.sin(angle)], axis=1).astype(jnp.bfloat16)


def taper_table():
    place = jnp.arange(TAPS * L, dtype=jnp.float32)
    offset = (place - TAPS * L / 2.0 + 0.5) / L
    window = 0.5 - 0.5 * jnp.cos(2.0 * math.pi * (place + 0.5) / (TAPS * L))
    return (jnp.sinc(offset) * window).reshape(TAPS, L)


def exchange(
    x_hbm, taper, table, k_out, turned, j_out, power, factor_col,
    xv, filt, spec, w, load_sem, hist_send, hist_recv, send_sem, recv_sem,
):
    wide = lax.axis_index("wide")
    narrow = lax.axis_index("narrow")
    x, y, z, core = wide // 4, (wide // 2) % 2 * 2 + narrow // 4, narrow % 4, wide % 2
    mine = wide * NARROW + narrow

    def partner(step):
        offset = (37 * step) % 128
        px = (x + (offset // 2) % 4) % 4
        py = (y + (offset // 8) % 4) % 4
        pz = (z + offset // 32) % 4
        pc = (core + offset % 2) % 2
        return px * 4 + py // 2 * 2 + pc, py % 2 * 4 + pz

    barrier = pltpu.get_barrier_semaphore()

    def greet(step, carry):
        pl.semaphore_signal(barrier, inc=1, device_id=partner(step), device_id_type=MESH)
        return carry

    lax.fori_loop(1, 128, greet, 0)

    loads = []
    ready = 0
    pieces = [(STEP - 3, 2 * STEP), (2 * STEP, 3 * STEP), (3 * STEP, 4 * STEP), (0, STEP - 3)]
    for index, (first, last) in enumerate(pieces):
        copy = pltpu.make_async_copy(
            x_hbm.at[:, first * L : last * L],
            xv.at[:, (first + 3) * L : (last + 3) * L],
            load_sem.at[index],
        )
        copy.start()
        loads.append(copy)

    history = pltpu.make_async_remote_copy(
        x_hbm.at[:, FR_DEV * L - HIST :],
        xv.at[:, :HIST],
        hist_send,
        hist_recv,
        device_id=(wide, (narrow + 1) % NARROW),
        device_id_type=MESH,
    )

    def compute(g):
        def pair(p, carry):
            for half in range(2):
                base = (g * STEP + 2 * p + half) * L
                for r in range(0, ROWS, 16):
                    total = None
                    for tap in range(TAPS):
                        part = xv[r : r + 16, pl.ds(pl.multiple_of(base + tap * L, L), L)]
                        term = part.astype(jnp.float32) * taper[tap : tap + 1, :]
                        total = term if total is None else total + term
                    filt[half * ROWS + r : half * ROWS + r + 16, :] = total.astype(jnp.bfloat16)
            out = lax.dot_general(
                table[...], filt[...], (((1,), (1,)), ((), ())), preferred_element_type=jnp.float32
            )
            row = pl.multiple_of(p * (2 * 2 * CHAN), 2 * 2 * CHAN)
            spec[pl.ds(row, 2 * CHAN), :] = out[:, :ROWS]
            spec[pl.ds(row + 2 * CHAN, 2 * CHAN), :] = out[:, ROWS:]
            return carry

        lax.fori_loop(0, STEP // 2, pair, 0)

        def turn(c, carry):
            re = spec[pl.ds(c, STEP, stride=2 * CHAN), :]
            im = spec[pl.ds(c + CHAN, STEP, stride=2 * CHAN), :]
            w[g, c] = jnp.concatenate([re, im], axis=0).astype(jnp.bfloat16)
            return carry

        lax.fori_loop(0, CHAN, turn, 0)

    def send(g):
        row = pl.multiple_of(narrow * (2 * STEP), 2 * STEP)
        col = pl.multiple_of(wide * ROWS, ROWS)
        dst = k_out.at[g, pl.ds(row, 2 * STEP), pl.ds(col, ROWS)]

        def one(step, carry):
            pw, pn = partner(step)
            pltpu.make_async_remote_copy(
                w.at[g, pw * NARROW + pn],
                dst,
                send_sem,
                recv_sem.at[g],
                device_id=(pw, pn),
                device_id_type=MESH,
            ).start()
            return carry

        lax.fori_loop(1, 128, one, 0)
        pltpu.make_async_copy(w.at[g, mine], dst, recv_sem.at[g]).start()

    for index, g in enumerate(ORDER):
        loads[index].wait()
        if g == 0:
            @pl.when(narrow > 0)
            def _():
                history.wait_recv()

        compute(g)
        if index == 0:
            pl.semaphore_wait(barrier, 127)

            @pl.when(narrow == 0)
            def _():
                xv[:, :HIST] = jnp.zeros((ROWS, HIST), jnp.bfloat16)

            @pl.when(narrow < NARROW - 1)
            def _():
                history.start()

        send(g)

    for index, g in enumerate(ORDER):
        pltpu.make_async_copy(k_out.at[g], k_out.at[g], recv_sem.at[g]).wait()

        def block(b, carry):
            cols = pl.ds(pl.multiple_of(b * TILE, TILE), TILE)
            value = k_out[g, :, cols]
            j_out[g, cols, :] = value.T
            sums = jnp.zeros((1, TILE), jnp.float32)
            for r in range(0, KB, 2 * STEP):
                re = value[r : r + STEP, :]
                im = value[r + STEP : r + 2 * STEP, :]
                turned[g, r : r + 2 * STEP, cols] = jnp.concatenate([-im, re], axis=0)
                both = value[r : r + 2 * STEP, :].astype(jnp.float32)
                sums = sums + jnp.sum(both * both, axis=0, keepdims=True)
            if index == 0:
                power[:, cols] = sums
            else:
                power[:, cols] = power[:, cols] + sums
            return carry

        lax.fori_loop(0, S // TILE, block, 0)

    factor = 1.0 / jnp.sqrt(power[...] / FRAMES + 1e-06)
    power[...] = factor
    for b in range(0, S, 128):
        factor_col[b : b + 128, :] = jnp.broadcast_to(factor[:, b : b + 128], (128, 128)).T

    @pl.when(narrow < NARROW - 1)
    def _():
        history.wait_send()

    for g in range(CHUNKS):
        part = w.at[g, pl.ds(0, 127)]
        pltpu.make_async_copy(part, part, send_sem).wait()


def correlate(k, turned, j, factor_row, factor_col, out, stage, sem):
    def rows(i, slot, wait):
        @pl.when(wait)
        def _():
            pltpu.make_async_copy(stage.at[slot], out.at[0, pl.ds(0, TILE), :], sem.at[slot]).wait()

        r = pl.ds(pl.multiple_of(i * TILE, TILE), TILE)
        left = [j[g, r, :] for g in range(CHUNKS)]
        scale = jnp.tile(factor_col[r, :], (1, TILE // 128)) * (1.0 / FRAMES)

        def product(right, cols):
            total = None
            for g in range(CHUNKS):
                term = jnp.dot(left[g], right[g, :, cols], preferred_element_type=jnp.float32)
                total = term if total is None else total + term
            return total * scale * factor_row[:, cols]

        def column(c, carry):
            cols = pl.ds(pl.multiple_of(c * TILE, TILE), TILE)

            @pl.when(c < i)
            def _():
                stage[slot, :, cols] = product(k, cols)

            @pl.when(c > i)
            def _():
                stage[slot, :, cols] = product(turned, cols)

            @pl.when(c == i)
            def _():
                row = lax.broadcasted_iota(jnp.int32, (TILE, TILE), 0)
                col = lax.broadcasted_iota(jnp.int32, (TILE, TILE), 1)
                stage[slot, :, cols] = jnp.where(row >= col, product(k, cols), product(turned, cols))

            return carry

        lax.fori_loop(0, S // TILE, column, 0)
        pltpu.make_async_copy(stage.at[slot], out.at[0, r, :], sem.at[slot]).start()

    def both(p, carry):
        rows(2 * p, 0, p > 0)
        rows(2 * p + 1, 1, p > 0)
        return carry

    lax.fori_loop(0, S // TILE // 2, both, 0)
    for slot in range(2):
        pltpu.make_async_copy(stage.at[slot], out.at[0, pl.ds(0, TILE), :], sem.at[slot]).wait()


def body(voltages):
    vmem = pl.BlockSpec(memory_space=pltpu.VMEM)
    hbm = pl.BlockSpec(memory_space=pl.ANY)
    dma = pltpu.SemaphoreType.DMA
    k, turned, j, power, factor_col = pl.pallas_call(
        exchange,
        out_shape=[
            pltpu.VMEM((CHUNKS, KB, S), jnp.bfloat16),
            pltpu.VMEM((CHUNKS, KB, S), jnp.bfloat16),
            pltpu.VMEM((CHUNKS, S, KB), jnp.bfloat16),
            pltpu.VMEM((1, S), jnp.float32),
            pltpu.VMEM((S, 128), jnp.float32),
        ],
        in_specs=[hbm, vmem, vmem],
        out_specs=[vmem] * 5,
        scratch_shapes=[
            pltpu.VMEM((ROWS, (FR_DEV + TAPS - 1) * L), jnp.bfloat16),
            pltpu.VMEM((2 * ROWS, L), jnp.bfloat16),
            pltpu.VMEM((STEP * 2 * CHAN, ROWS), jnp.float32),
            pltpu.VMEM((CHUNKS, CHAN, 2 * STEP, ROWS), jnp.bfloat16),
            dma((CHUNKS,)),
            dma,
            dma,
            dma,
            dma((CHUNKS,)),
        ],
        compiler_params=pltpu.CompilerParams(
            collective_id=0, has_side_effects=True, vmem_limit_bytes=34 << 20
        ),
        name="exchange",
    )(voltages, taper_table(), channel_table(CHAN).T)
    return pl.pallas_call(
        correlate,
        out_shape=jax.ShapeDtypeStruct((1, S, S), jnp.float32),
        in_specs=[vmem] * 5,
        out_specs=hbm,
        scratch_shapes=[pltpu.VMEM((2, TILE, S), jnp.float32), dma((2,))],
        compiler_params=pltpu.CompilerParams(vmem_limit_bytes=34 << 20),
        name="correlate",
    )(k, turned, j, power, factor_col)


def solution(mesh):
    return jax.shard_map(
        body,
        mesh=mesh,
        in_specs=(P("wide", "narrow"),),
        out_specs=P(("wide", "narrow"), None, None),
        check_vma=False,
    )
```

```python
import functools
import math

import jax
import jax.numpy as jnp
from jax import lax
from jax.experimental import pallas as pl
from jax.experimental.pallas import tpu as pltpu
from jax.sharding import PartitionSpec as P

S = 2048
L = 512
TAPS = 4
CHAN = 128
FRAMES = 512
WIDE = 16
NARROW = 8
ROWS = S // WIDE
FR_DEV = FRAMES // NARROW
STEP = 16
CHUNKS = FR_DEV // STEP
ORDER = (1, 2, 3, 0)
KB = 2 * STEP * NARROW
TILE = 256
MESH = pl.DeviceIdType.MESH


def channel_table(count):
    index = jnp.arange(L, dtype=jnp.int32)[:, None]
    channel = jnp.arange(count, dtype=jnp.int32)[None, :]
    angle = (index * channel % L).astype(jnp.float32) * (2.0 * math.pi / L)
    return jnp.concatenate([jnp.cos(angle), -jnp.sin(angle)], axis=1).astype(jnp.bfloat16)


def taper_table():
    place = jnp.arange(TAPS * L, dtype=jnp.float32)
    offset = (place - TAPS * L / 2.0 + 0.5) / L
    window = 0.5 - 0.5 * jnp.cos(2.0 * math.pi * (place + 0.5) / (TAPS * L))
    return (jnp.sinc(offset) * window).reshape(TAPS, L)


def products(i, left, right, emit):
    def dot(kind, cols):
        return jnp.dot(left, right[kind, :, cols], preferred_element_type=jnp.float32)

    def columns(c):
        return pl.ds(pl.multiple_of(c * TILE, TILE), TILE)

    for t in range(1, S // TILE):
        c = (i + t) % (S // TILE)
        emit(columns(c), dot(jnp.where(c > i, 1, 0), columns(c)))
    row = lax.broadcasted_iota(jnp.int32, (TILE, TILE), 0)
    col = lax.broadcasted_iota(jnp.int32, (TILE, TILE), 1)
    emit(columns(i), jnp.where(row >= col, dot(0, columns(i)), dot(1, columns(i))))


def exchange(
    x_hbm, taper, table, acc, last, last_j, power, factor_col,
    xv, filt, spec, w, kt, j, taper_edge, load_sem, hist_send, hist_recv, send_sem, recv_sem,
):
    wide = lax.axis_index("wide")
    narrow = lax.axis_index("narrow")
    x, y, z, core = wide // 4, (wide // 2) % 2 * 2 + narrow // 4, narrow % 4, wide % 2
    mine = wide * NARROW + narrow

    def partners(q):
        for step in range(4):
            dy = (q % 4 + step) % 4
            px = (x + step) % 4
            py = (y + dy) % 4
            pz = (z + q // 4 + dy + step) % 4
            for flip in range(2):
                pc = (core + flip) % 2
                yield step == 0 and flip == 0, (px * 4 + py // 2 * 2 + pc, py % 2 * 4 + pz)

    def everyone(q, visit):
        for own, device in partners(q):
            if own:
                pl.when(q > 0)(functools.partial(visit, device))
            else:
                visit(device)

    barrier = pltpu.get_barrier_semaphore()

    def greet(q, carry):
        def signal(device):
            pl.semaphore_signal(barrier, inc=1, device_id=device, device_id_type=MESH)

        everyone(q, signal)
        return carry

    lax.fori_loop(0, 16, greet, 0)

    loads = []
    pieces = [(STEP - 3, 2 * STEP), (2 * STEP, 3 * STEP), (3 * STEP, 4 * STEP), (0, STEP - 3)]
    for index, (first, end) in enumerate(pieces):
        copy = pltpu.make_async_copy(
            x_hbm.at[:, first * L : end * L],
            xv.at[:, (first + 2) * L : (end + 2) * L],
            load_sem.at[index],
        )
        copy.start()
        loads.append(copy)

    taper_edge[...] = taper[...] * jnp.where(
        (narrow == NARROW - 1) & (lax.broadcasted_iota(jnp.int32, (TAPS, L), 0) < TAPS - 1), 0.0, 1.0
    )

    def ahead(r):
        return pltpu.make_async_remote_copy(
            x_hbm.at[pl.ds(r, 16), (FR_DEV - 2) * L :],
            xv.at[pl.ds(r, 16), : 2 * L],
            hist_send.at[0],
            hist_recv.at[0],
            device_id=(wide, (narrow + 1) % NARROW),
            device_id_type=MESH,
        )

    def back(r):
        return pltpu.make_async_remote_copy(
            x_hbm.at[pl.ds(r, 16), :L],
            xv.at[pl.ds(r, 16), (FR_DEV + 2) * L :],
            hist_send.at[1],
            hist_recv.at[1],
            device_id=(wide, (narrow + NARROW - 1) % NARROW),
            device_id_type=MESH,
        )

    def compute(g):
        def filtered(slot, half, base, weights):
            for r in range(0, ROWS, 16):
                total = None
                for tap in range(TAPS):
                    part = xv[r : r + 16, pl.ds(pl.multiple_of(base + tap * L, L), L)]
                    term = part.astype(jnp.float32) * weights[tap : tap + 1, :]
                    total = term if total is None else total + term
                filt[slot, half * ROWS + r : half * ROWS + r + 16, :] = total.astype(jnp.bfloat16)

        def group(p, carry):
            for slot in range(2):
                for half in range(2):
                    f = g * STEP + 4 * p + 2 * slot + half
                    filtered(slot, half, jnp.maximum(f - 1, 0) * L, taper)
                if g == 0 and slot == 0:

                    @pl.when(p == 0)
                    def _():
                        filtered(0, 0, (FR_DEV - 1) * L, taper_edge)

                out = lax.dot_general(
                    table[...], filt[slot], (((1,), (1,)), ((), ())), preferred_element_type=jnp.float32
                )
                row = pl.multiple_of((4 * p + 2 * slot) * (2 * CHAN), 2 * 2 * CHAN)
                spec[pl.ds(row, 2 * CHAN), :] = out[:, :ROWS]
                spec[pl.ds(row + 2 * CHAN, 2 * CHAN), :] = out[:, ROWS:]
            return carry

        lax.fori_loop(0, STEP // 4, group, 0)

        def turn(b, carry):
            for c in range(8):
                re = spec[pl.ds(8 * b + c, STEP, stride=2 * CHAN), :]
                im = spec[pl.ds(8 * b + c + CHAN, STEP, stride=2 * CHAN), :]
                w[g, 8 * b + c] = jnp.concatenate([re, im], axis=0).astype(jnp.bfloat16)
            return carry

        lax.fori_loop(0, CHAN // 8, turn, 0)

    def landing(g):
        return kt.at[g - 1, 0] if g > 0 else last.at[0]

    def send(g, history):
        row = pl.multiple_of(narrow * (2 * STEP), 2 * STEP)
        col = pl.multiple_of(wide * ROWS, ROWS)
        dst = landing(g).at[pl.ds(row, 2 * STEP), pl.ds(col, ROWS)]

        def one(q, carry):
            if history:
                r = pl.multiple_of(q % 8 * 16, 16)

                @pl.when((narrow < NARROW - 1) & (q < 8))
                def _():
                    ahead(r).start()

                @pl.when(q >= 8)
                def _():
                    back(r).start()

            def start(device):
                pltpu.make_async_remote_copy(
                    w.at[g, device[0] * NARROW + device[1]],
                    dst,
                    send_sem,
                    recv_sem.at[g],
                    device_id=device,
                    device_id_type=MESH,
                ).start()

            everyone(q, start)
            return carry

        lax.fori_loop(0, 16, one, 0)
        pltpu.make_async_copy(w.at[g, mine], dst, recv_sem.at[g]).start()

    for index, g in enumerate(ORDER):
        loads[index].wait()
        if g == 0:
            before = xv.at[:, : 2 * L]
            after = xv.at[:, (FR_DEV + 2) * L :]

            @pl.when(narrow > 0)
            def _():
                pltpu.make_async_copy(before, before, hist_recv.at[0]).wait()

            pltpu.make_async_copy(after, after, hist_recv.at[1]).wait()

        compute(g)
        if index == 0:
            pl.semaphore_wait(barrier, 127)

            @pl.when(narrow == 0)
            def _():
                xv[:, : 2 * L] = jnp.zeros((ROWS, 2 * L), jnp.bfloat16)

        send(g, index == 0)

    for index, g in enumerate(ORDER):
        right = last if g == 0 else kt.at[g - 1]
        left = last_j if g == 0 else j
        pltpu.make_async_copy(right.at[0], right.at[0], recv_sem.at[g]).wait()

        def block(b, carry):
            cols = pl.ds(pl.multiple_of(b * TILE, TILE), TILE)
            value = right[0, :, cols]
            left[cols, :] = value.T
            sums = jnp.zeros((1, TILE), jnp.float32)
            for r in range(0, KB, 2 * STEP):
                re = value[r : r + STEP, :]
                im = value[r + STEP : r + 2 * STEP, :]
                right[1, r : r + 2 * STEP, cols] = jnp.concatenate([-im, re], axis=0)
                both = value[r : r + 2 * STEP, :].astype(jnp.float32)
                sums = sums + jnp.sum(both * both, axis=0, keepdims=True)
            if index == 0:
                power[:, cols] = sums
            else:
                power[:, cols] = power[:, cols] + sums
            return carry

        lax.fori_loop(0, S // TILE, block, 0)

        if g == 0:
            break

        def rows(i, carry):
            r = pl.ds(pl.multiple_of(i * TILE, TILE), TILE)

            def emit(cols, value):
                acc[r, cols] = value if index == 0 else acc[r, cols] + value

            products(i, j[r, :], right, emit)
            return carry

        lax.fori_loop(0, S // TILE, rows, 0)

    factor = 1.0 / jnp.sqrt(power[...] / FRAMES + 1e-06)
    power[...] = factor
    for b in range(0, S, 128):
        factor_col[b : b + 128, :] = jnp.broadcast_to(factor[:, b : b + 128], (128, 128)).T

    @pl.when(narrow < NARROW - 1)
    def _():
        sent = x_hbm.at[:, : 2 * L]
        pltpu.make_async_copy(sent, sent, hist_send.at[0]).wait()

    sent = x_hbm.at[:, :L]
    pltpu.make_async_copy(sent, sent, hist_send.at[1]).wait()
    for g in range(CHUNKS):
        part = w.at[g, pl.ds(0, 127)]
        pltpu.make_async_copy(part, part, send_sem).wait()


def finish(acc, last, last_j, factor_row, factor_col, out, stage, sem):
    def arrival(slot):
        return pltpu.make_async_copy(stage.at[slot], out.at[0, pl.ds(0, TILE), :], sem.at[slot])

    def rows(i, slot, wait):
        pl.when(wait)(lambda: arrival(slot).wait())
        r = pl.ds(pl.multiple_of(i * TILE, TILE), TILE)
        scale = jnp.tile(factor_col[r, :], (1, TILE // 128)) * (1.0 / FRAMES)

        def emit(cols, value):
            stage[slot, :, cols] = (acc[r, cols] + value) * scale * factor_row[:, cols]

        products(i, last_j[r, :], last, emit)
        pltpu.make_async_copy(stage.at[slot], out.at[0, r, :], sem.at[slot]).start()

    def both(p, carry):
        rows(2 * p, 0, p > 0)
        rows(2 * p + 1, 1, p > 0)
        return carry

    lax.fori_loop(0, S // TILE // 2, both, 0)
    for slot in range(2):
        arrival(slot).wait()


def body(voltages):
    vmem = pl.BlockSpec(memory_space=pltpu.VMEM)
    hbm = pl.BlockSpec(memory_space=pl.ANY)
    dma = pltpu.SemaphoreType.DMA
    parts = pl.pallas_call(
        exchange,
        out_shape=[
            pltpu.VMEM((S, S), jnp.float32),
            pltpu.VMEM((2, KB, S), jnp.bfloat16),
            pltpu.VMEM((S, KB), jnp.bfloat16),
            pltpu.VMEM((1, S), jnp.float32),
            pltpu.VMEM((S, 128), jnp.float32),
        ],
        in_specs=[hbm, vmem, vmem],
        out_specs=[vmem] * 5,
        scratch_shapes=[
            pltpu.VMEM((ROWS, (FR_DEV + TAPS - 1) * L), jnp.bfloat16),
            pltpu.VMEM((2, 2 * ROWS, L), jnp.bfloat16),
            pltpu.VMEM((STEP * 2 * CHAN, ROWS), jnp.float32),
            pltpu.VMEM((CHUNKS, CHAN, 2 * STEP, ROWS), jnp.bfloat16),
            pltpu.VMEM((CHUNKS - 1, 2, KB, S), jnp.bfloat16),
            pltpu.VMEM((S, KB), jnp.bfloat16),
            pltpu.VMEM((TAPS, L), jnp.float32),
            dma((CHUNKS,)),
            dma((2,)),
            dma((2,)),
            dma,
            dma((CHUNKS,)),
        ],
        compiler_params=pltpu.CompilerParams(
            collective_id=0, has_side_effects=True, vmem_limit_bytes=32 << 20
        ),
        name="exchange",
    )(voltages, taper_table(), channel_table(CHAN).T)
    return pl.pallas_call(
        finish,
        out_shape=jax.ShapeDtypeStruct((1, S, S), jnp.float32),
        in_specs=[vmem] * 5,
        out_specs=hbm,
        scratch_shapes=[pltpu.VMEM((2, TILE, S), jnp.float32), dma((2,))],
        compiler_params=pltpu.CompilerParams(vmem_limit_bytes=6 << 20),
        name="finish",
    )(*parts)


def solution(mesh):
    return jax.shard_map(
        body,
        mesh=mesh,
        in_specs=(P("wide", "narrow"),),
        out_specs=P(("wide", "narrow"), None, None),
        check_vma=False,
    )
```

```python
import functools
import math

import jax
import jax.numpy as jnp
from jax import lax
from jax.experimental import pallas as pl
from jax.experimental.pallas import tpu as pltpu
from jax.sharding import PartitionSpec as P

S = 2048
L = 512
TAPS = 4
CHAN = 128
FRAMES = 512
WIDE = 16
NARROW = 8
ROWS = S // WIDE
FR_DEV = FRAMES // NARROW
STEP = 16
CHUNKS = FR_DEV // STEP
ORDER = (1, 2, 3, 0)
KB = 2 * STEP * NARROW
TILE = 256
MESH = pl.DeviceIdType.MESH


def channel_table():
    index = lax.broadcasted_iota(jnp.int32, (CHAN, L), 1)
    channel = lax.broadcasted_iota(jnp.int32, (CHAN, L), 0)
    angle = (index * channel % L).astype(jnp.float32) * (2.0 * math.pi / L)
    return jnp.concatenate([jnp.cos(angle), -jnp.sin(angle)], axis=0).astype(jnp.bfloat16)


def taper_table():
    tap = lax.broadcasted_iota(jnp.int32, (TAPS, L), 0)
    place = (tap * L + lax.broadcasted_iota(jnp.int32, (TAPS, L), 1)).astype(jnp.float32)
    offset = (place - TAPS * L / 2.0 + 0.5) * (math.pi / L)
    window = 0.5 - 0.5 * jnp.cos(2.0 * math.pi * (place + 0.5) / (TAPS * L))
    return jnp.sin(offset) / offset * window


def make_chunk(g, xv, taper, taper_edge, table, filt, spec, w):
    def filtered(slot, half, base, weights):
        for r in range(0, ROWS, 16):
            total = None
            for tap in range(TAPS):
                part = xv[r : r + 16, pl.ds(pl.multiple_of(base + tap * L, L), L)]
                term = part.astype(jnp.float32) * weights[tap : tap + 1, :]
                total = term if total is None else total + term
            filt[slot, half * ROWS + r : half * ROWS + r + 16, :] = total.astype(jnp.bfloat16)

    def group(p, carry):
        for slot in range(2):
            for half in range(2):
                f = g * STEP + 4 * p + 2 * slot + half
                filtered(slot, half, jnp.maximum(f - 1, 0) * L, taper)
            if g == 0 and slot == 0:

                @pl.when(p == 0)
                def _():
                    filtered(0, 0, (FR_DEV - 1) * L, taper_edge)

            out = lax.dot_general(
                table[...], filt[slot], (((1,), (1,)), ((), ())), preferred_element_type=jnp.float32
            )
            row = pl.multiple_of((4 * p + 2 * slot) * (2 * CHAN), 2 * 2 * CHAN)
            spec[pl.ds(row, 2 * CHAN), :] = out[:, :ROWS]
            spec[pl.ds(row + 2 * CHAN, 2 * CHAN), :] = out[:, ROWS:]
        return carry

    lax.fori_loop(0, STEP // 4, group, 0)

    def turn(b, carry):
        for c in range(8):
            re = spec[pl.ds(8 * b + c, STEP, stride=2 * CHAN), :]
            im = spec[pl.ds(8 * b + c + CHAN, STEP, stride=2 * CHAN), :]
            w[8 * b + c] = jnp.concatenate([re, im], axis=0).astype(jnp.bfloat16)
        return carry

    lax.fori_loop(0, CHAN // 8, turn, 0)


def prepare(
    x_hbm, xv, taper, table, w, filt, spec, load_sem, send_sem, recv_sem,
):
    wide = lax.axis_index("wide")
    narrow = lax.axis_index("narrow")
    after = (wide, (narrow + 1) % NARROW)
    before = (wide, (narrow + NARROW - 1) % NARROW)
    barrier = pltpu.get_barrier_semaphore()
    for device in (after, before):
        pl.semaphore_signal(barrier, inc=1, device_id=device, device_id_type=MESH)

    first = ORDER[0]
    pieces = [(first * STEP - 3, first * STEP + STEP), (0, first * STEP - 3), (first * STEP + STEP, FR_DEV)]
    loads = [
        pltpu.make_async_copy(
            x_hbm.at[:, begin * L : end * L], xv.at[:, (begin + 2) * L : (end + 2) * L], load_sem.at[index]
        )
        for index, (begin, end) in enumerate(pieces)
    ]
    loads[0].start()
    pl.semaphore_wait(barrier, 2)
    ahead = pltpu.make_async_remote_copy(
        x_hbm.at[:, (FR_DEV - 2) * L :],
        xv.at[:, : 2 * L],
        send_sem.at[0],
        recv_sem.at[0],
        device_id=after,
        device_id_type=MESH,
    )
    back = pltpu.make_async_remote_copy(
        x_hbm.at[:, :L],
        xv.at[:, (FR_DEV + 2) * L :],
        send_sem.at[1],
        recv_sem.at[1],
        device_id=before,
        device_id_type=MESH,
    )
    ahead.start()
    back.start()
    loads[1].start()
    loads[2].start()
    taper[...] = taper_table()
    table[...] = channel_table()
    loads[0].wait()
    make_chunk(first, xv, taper, None, table, filt, spec, w)
    loads[1].wait()
    loads[2].wait()
    ahead.wait()
    back.wait()

    @pl.when(narrow == 0)
    def _():
        xv[:, : 2 * L] = jnp.zeros((ROWS, 2 * L), jnp.bfloat16)


def products(i, left, right, emit):
    def dot(kind, cols):
        return jnp.dot(left, right[kind, :, cols], preferred_element_type=jnp.float32)

    def columns(c):
        return pl.ds(pl.multiple_of(c * TILE, TILE), TILE)

    for t in range(1, S // TILE):
        c = (i + t) % (S // TILE)
        emit(columns(c), dot(jnp.where(c > i, 1, 0), columns(c)))
    row = lax.broadcasted_iota(jnp.int32, (TILE, TILE), 0)
    col = lax.broadcasted_iota(jnp.int32, (TILE, TILE), 1)
    emit(columns(i), jnp.where(row >= col, dot(0, columns(i)), dot(1, columns(i))))


def exchange(
    xv, taper, table, w_first, acc, last, last_j, power, factor_col,
    filt, spec, w, kt, j, taper_edge, send_sem, recv_sem,
):
    wide = lax.axis_index("wide")
    narrow = lax.axis_index("narrow")
    x, y, z, core = wide // 4, (wide // 2) % 2 * 2 + narrow // 4, narrow % 4, wide % 2
    mine = wide * NARROW + narrow

    def partners(q):
        for step in range(4):
            dy = (q % 4 + step) % 4
            px = (x + step) % 4
            py = (y + dy) % 4
            pz = (z + q // 4 + dy + step) % 4
            for flip in range(2):
                pc = (core + flip) % 2
                yield step == 0 and flip == 0, (px * 4 + py // 2 * 2 + pc, py % 2 * 4 + pz)

    def everyone(q, visit):
        for own, device in partners(q):
            if own:
                pl.when(q > 0)(functools.partial(visit, device))
            else:
                visit(device)

    barrier = pltpu.get_barrier_semaphore()

    def greet(q, carry):
        def signal(device):
            pl.semaphore_signal(barrier, inc=1, device_id=device, device_id_type=MESH)

        everyone(q, signal)
        return carry

    lax.fori_loop(0, 16, greet, 0)

    taper_edge[...] = taper[...] * jnp.where(
        (narrow == NARROW - 1) & (lax.broadcasted_iota(jnp.int32, (TAPS, L), 0) < TAPS - 1), 0.0, 1.0
    )

    def chunk(g):
        return w_first if g == ORDER[0] else w.at[ORDER.index(g) - 1]

    def landing(g):
        return kt.at[g - 1, 0] if g > 0 else last.at[0]

    def send(g):
        row = pl.multiple_of(narrow * (2 * STEP), 2 * STEP)
        col = pl.multiple_of(wide * ROWS, ROWS)
        dst = landing(g).at[pl.ds(row, 2 * STEP), pl.ds(col, ROWS)]

        def one(q, carry):
            def start(device):
                pltpu.make_async_remote_copy(
                    chunk(g).at[device[0] * NARROW + device[1]],
                    dst,
                    send_sem,
                    recv_sem.at[g],
                    device_id=device,
                    device_id_type=MESH,
                ).start()

            everyone(q, start)
            return carry

        lax.fori_loop(0, 16, one, 0)
        pltpu.make_async_copy(chunk(g).at[mine], dst, recv_sem.at[g]).start()

    pl.semaphore_wait(barrier, 127)
    send(ORDER[0])
    for g in ORDER[1:]:
        make_chunk(g, xv, taper, taper_edge, table, filt, spec, chunk(g))
        send(g)

    for index, g in enumerate(ORDER):
        right = last if g == 0 else kt.at[g - 1]
        left = last_j if g == 0 else j
        pltpu.make_async_copy(right.at[0], right.at[0], recv_sem.at[g]).wait()

        def block(b, carry):
            cols = pl.ds(pl.multiple_of(b * TILE, TILE), TILE)
            value = right[0, :, cols]
            left[cols, :] = value.T
            sums = jnp.zeros((1, TILE), jnp.float32)
            for r in range(0, KB, 2 * STEP):
                re = value[r : r + STEP, :]
                im = value[r + STEP : r + 2 * STEP, :]
                right[1, r : r + 2 * STEP, cols] = jnp.concatenate([-im, re], axis=0)
                both = value[r : r + 2 * STEP, :].astype(jnp.float32)
                sums = sums + jnp.sum(both * both, axis=0, keepdims=True)
            if index == 0:
                power[:, cols] = sums
            else:
                power[:, cols] = power[:, cols] + sums
            return carry

        lax.fori_loop(0, S // TILE, block, 0)

        if g == 0:
            break

        def rows(i, carry):
            r = pl.ds(pl.multiple_of(i * TILE, TILE), TILE)

            def emit(cols, value):
                acc[r, cols] = value if index == 0 else acc[r, cols] + value

            products(i, j[r, :], right, emit)
            return carry

        lax.fori_loop(0, S // TILE, rows, 0)

    factor = 1.0 / jnp.sqrt(power[...] / FRAMES + 1e-06)
    power[...] = factor
    for b in range(0, S, 128):
        factor_col[b : b + 128, :] = jnp.broadcast_to(factor[:, b : b + 128], (128, 128)).T

    for g in range(CHUNKS):
        part = chunk(g).at[pl.ds(0, 127)]
        pltpu.make_async_copy(part, part, send_sem).wait()


def finish(acc, last, last_j, factor_row, factor_col, out, stage, sem):
    def arrival(slot):
        return pltpu.make_async_copy(stage.at[slot], out.at[0, pl.ds(0, TILE), :], sem.at[slot])

    def rows(i, slot, wait):
        pl.when(wait)(lambda: arrival(slot).wait())
        r = pl.ds(pl.multiple_of(i * TILE, TILE), TILE)
        scale = jnp.tile(factor_col[r, :], (1, TILE // 128)) * (1.0 / FRAMES)

        def emit(cols, value):
            stage[slot, :, cols] = (acc[r, cols] + value) * scale * factor_row[:, cols]

        products(i, last_j[r, :], last, emit)
        pltpu.make_async_copy(stage.at[slot], out.at[0, r, :], sem.at[slot]).start()

    def both(p, carry):
        rows(2 * p, 0, p > 0)
        rows(2 * p + 1, 1, p > 0)
        return carry

    lax.fori_loop(0, S // TILE // 2, both, 0)
    for slot in range(2):
        arrival(slot).wait()


def body(voltages):
    vmem = pl.BlockSpec(memory_space=pltpu.VMEM)
    hbm = pl.BlockSpec(memory_space=pl.ANY)
    dma = pltpu.SemaphoreType.DMA
    work = [
        pltpu.VMEM((2, 2 * ROWS, L), jnp.bfloat16),
        pltpu.VMEM((STEP * 2 * CHAN, ROWS), jnp.float32),
    ]
    prepared = pl.pallas_call(
        prepare,
        out_shape=[
            pltpu.VMEM((ROWS, (FR_DEV + TAPS - 1) * L), jnp.bfloat16),
            pltpu.VMEM((TAPS, L), jnp.float32),
            pltpu.VMEM((2 * CHAN, L), jnp.bfloat16),
            pltpu.VMEM((CHAN, 2 * STEP, ROWS), jnp.bfloat16),
        ],
        in_specs=[hbm],
        out_specs=[vmem] * 4,
        scratch_shapes=[*work, dma((3,)), dma((2,)), dma((2,))],
        compiler_params=pltpu.CompilerParams(
            collective_id=1, has_side_effects=True, vmem_limit_bytes=48 << 20
        ),
        name="prepare",
    )(voltages)
    parts = pl.pallas_call(
        exchange,
        out_shape=[
            pltpu.VMEM((S, S), jnp.float32),
            pltpu.VMEM((2, KB, S), jnp.bfloat16),
            pltpu.VMEM((S, KB), jnp.bfloat16),
            pltpu.VMEM((1, S), jnp.float32),
            pltpu.VMEM((S, 128), jnp.float32),
        ],
        in_specs=[vmem] * 4,
        out_specs=[vmem] * 5,
        scratch_shapes=[
            *work,
            pltpu.VMEM((CHUNKS - 1, CHAN, 2 * STEP, ROWS), jnp.bfloat16),
            pltpu.VMEM((CHUNKS - 1, 2, KB, S), jnp.bfloat16),
            pltpu.VMEM((S, KB), jnp.bfloat16),
            pltpu.VMEM((TAPS, L), jnp.float32),
            dma,
            dma((CHUNKS,)),
        ],
        compiler_params=pltpu.CompilerParams(
            collective_id=0, has_side_effects=True, vmem_limit_bytes=18 << 20
        ),
        name="exchange",
    )(*prepared)
    return pl.pallas_call(
        finish,
        out_shape=jax.ShapeDtypeStruct((1, S, S), jnp.float32),
        in_specs=[vmem] * 5,
        out_specs=hbm,
        scratch_shapes=[pltpu.VMEM((2, TILE, S), jnp.float32), dma((2,))],
        compiler_params=pltpu.CompilerParams(vmem_limit_bytes=6 << 20),
        name="finish",
    )(*parts)


def solution(mesh):
    return jax.shard_map(
        body,
        mesh=mesh,
        in_specs=(P("wide", "narrow"),),
        out_specs=P(("wide", "narrow"), None, None),
        check_vma=False,
    )
```

```python
import functools
import math

import jax
import jax.numpy as jnp
from jax import lax
from jax.experimental import pallas as pl
from jax.experimental.pallas import tpu as pltpu
from jax.sharding import PartitionSpec as P

S = 2048
L = 512
TAPS = 4
CHAN = 128
FRAMES = 512
WIDE = 16
NARROW = 8
ROWS = S // WIDE
FR_DEV = FRAMES // NARROW
STEP = 16
CHUNKS = FR_DEV // STEP
ORDER = (1, 2, 3, 0)
KB = 2 * STEP * NARROW
TILE = 256
SLOTS = 4
MESH = pl.DeviceIdType.MESH


def channel_table():
    index = lax.broadcasted_iota(jnp.int32, (CHAN, L), 1)
    channel = lax.broadcasted_iota(jnp.int32, (CHAN, L), 0)
    angle = (index * channel % L).astype(jnp.float32) * (2.0 * math.pi / L)
    return jnp.concatenate([jnp.cos(angle), -jnp.sin(angle)], axis=0).astype(jnp.bfloat16)


def taper_table():
    tap = lax.broadcasted_iota(jnp.int32, (TAPS, L), 0)
    place = (tap * L + lax.broadcasted_iota(jnp.int32, (TAPS, L), 1)).astype(jnp.float32)
    offset = (place - TAPS * L / 2.0 + 0.5) * (math.pi / L)
    window = 0.5 - 0.5 * jnp.cos(2.0 * math.pi * (place + 0.5) / (TAPS * L))
    return jnp.sin(offset) / offset * window


def make_chunk(g, xv, taper, taper_edge, table, filt, spec, w):
    def filtered(slot, half, base, weights):
        for r in range(0, ROWS, 16):
            total = None
            for tap in range(TAPS):
                part = xv[r : r + 16, pl.ds(pl.multiple_of(base + tap * L, L), L)]
                term = part.astype(jnp.float32) * weights[tap : tap + 1, :]
                total = term if total is None else total + term
            filt[slot, half * ROWS + r : half * ROWS + r + 16, :] = total.astype(jnp.bfloat16)

    def group(p, carry):
        for slot in range(2):
            for half in range(2):
                f = g * STEP + 4 * p + 2 * slot + half
                filtered(slot, half, jnp.maximum(f - 1, 0) * L, taper)
            if g == 0 and slot == 0:

                @pl.when(p == 0)
                def _():
                    filtered(0, 0, (FR_DEV - 1) * L, taper_edge)

            out = lax.dot_general(
                table[...], filt[slot], (((1,), (1,)), ((), ())), preferred_element_type=jnp.float32
            )
            row = pl.multiple_of((4 * p + 2 * slot) * (2 * CHAN), 2 * 2 * CHAN)
            spec[pl.ds(row, 2 * CHAN), :] = out[:, :ROWS]
            spec[pl.ds(row + 2 * CHAN, 2 * CHAN), :] = out[:, ROWS:]
        return carry

    lax.fori_loop(0, STEP // 4, group, 0)

    def turn(b, carry):
        for c in range(8):
            re = spec[pl.ds(8 * b + c, STEP, stride=2 * CHAN), :]
            im = spec[pl.ds(8 * b + c + CHAN, STEP, stride=2 * CHAN), :]
            w[8 * b + c] = jnp.concatenate([re, im], axis=0).astype(jnp.bfloat16)
        return carry

    lax.fori_loop(0, CHAN // 8, turn, 0)


def products(i, left, right, emit):
    def dot(kind, cols):
        return jnp.dot(left, right[kind, :, cols], preferred_element_type=jnp.float32)

    def columns(c):
        return pl.ds(pl.multiple_of(c * TILE, TILE), TILE)

    for t in range(1, S // TILE):
        c = (i + t) % (S // TILE)
        emit(columns(c), dot(jnp.where(c > i, 1, 0), columns(c)))
    row = lax.broadcasted_iota(jnp.int32, (TILE, TILE), 0)
    col = lax.broadcasted_iota(jnp.int32, (TILE, TILE), 1)
    emit(columns(i), jnp.where(row >= col, dot(0, columns(i)), dot(1, columns(i))))


def exchange(
    x_hbm, acc, last, last_j, power, factor_col,
    xv, taper, taper_edge, table, filt, spec, w, kt, j, load_sem, edge_send, edge_recv, send_sem, recv_sem,
):
    wide = lax.axis_index("wide")
    narrow = lax.axis_index("narrow")
    x, y, z, core = wide // 4, (wide // 2) % 2 * 2 + narrow // 4, narrow % 4, wide % 2
    mine = wide * NARROW + narrow

    def partners(q):
        for step in range(4):
            dy = (q % 4 + step) % 4
            px = (x + step) % 4
            py = (y + dy) % 4
            pz = (z + q // 4 + dy + step) % 4
            for flip in range(2):
                pc = (core + flip) % 2
                yield step == 0 and flip == 0, (px * 4 + py // 2 * 2 + pc, py % 2 * 4 + pz)

    def everyone(q, visit):
        for own, device in partners(q):
            if own:
                pl.when(q > 0)(functools.partial(visit, device))
            else:
                visit(device)

    barrier = pltpu.get_barrier_semaphore()

    def greet(q, carry):
        def signal(device):
            pl.semaphore_signal(barrier, inc=1, device_id=device, device_id_type=MESH)

        everyone(q, signal)
        return carry

    lax.fori_loop(0, 16, greet, 0)

    first = ORDER[0]
    pieces = [(first * STEP - 3, first * STEP + STEP), (first * STEP + STEP, FR_DEV), (0, first * STEP - 3)]
    loads = [
        pltpu.make_async_copy(
            x_hbm.at[:, begin * L : end * L], xv.at[:, (begin + 2) * L : (end + 2) * L], load_sem.at[index]
        )
        for index, (begin, end) in enumerate(pieces)
    ]
    for copy in loads:
        copy.start()
    taper[...] = taper_table()
    table[...] = channel_table()
    taper_edge[...] = taper[...] * jnp.where(
        (narrow == NARROW - 1) & (lax.broadcasted_iota(jnp.int32, (TAPS, L), 0) < TAPS - 1), 0.0, 1.0
    )

    ahead = pltpu.make_async_remote_copy(
        x_hbm.at[:, (FR_DEV - 2) * L :],
        xv.at[:, : 2 * L],
        edge_send.at[0],
        edge_recv.at[0],
        device_id=(wide, (narrow + 1) % NARROW),
        device_id_type=MESH,
    )
    back = pltpu.make_async_remote_copy(
        x_hbm.at[:, :L],
        xv.at[:, (FR_DEV + 2) * L :],
        edge_send.at[1],
        edge_recv.at[1],
        device_id=(wide, (narrow + NARROW - 1) % NARROW),
        device_id_type=MESH,
    )

    def landing(g):
        return kt.at[g - 1, 0] if g > 0 else last.at[0]

    def send(g):
        row = pl.multiple_of(narrow * (2 * STEP), 2 * STEP)
        col = pl.multiple_of(wide * ROWS, ROWS)
        dst = landing(g).at[pl.ds(row, 2 * STEP), pl.ds(col, ROWS)]

        def one(q, carry):
            def start(device):
                pltpu.make_async_remote_copy(
                    w.at[g, device[0] * NARROW + device[1]],
                    dst,
                    send_sem,
                    recv_sem.at[g],
                    device_id=device,
                    device_id_type=MESH,
                ).start()

            everyone(q, start)
            return carry

        lax.fori_loop(0, 16, one, 0)
        pltpu.make_async_copy(w.at[g, mine], dst, recv_sem.at[g]).start()

    pl.semaphore_wait(barrier, 127)
    ahead.start()
    back.start()
    for index, g in enumerate(ORDER):
        if index < len(loads):
            loads[index].wait()
        make_chunk(g, xv, taper, taper_edge, table, filt, spec, w.at[g])
        if index == 0:
            ahead.wait()
            back.wait()

            @pl.when(narrow == 0)
            def _():
                xv[:, : 2 * L] = jnp.zeros((ROWS, 2 * L), jnp.bfloat16)

        send(g)

    for index, g in enumerate(ORDER):
        right = last if g == 0 else kt.at[g - 1]
        left = last_j if g == 0 else j
        pltpu.make_async_copy(right.at[0], right.at[0], recv_sem.at[g]).wait()

        def block(b, carry):
            cols = pl.ds(pl.multiple_of(b * TILE, TILE), TILE)
            value = right[0, :, cols]
            left[cols, :] = value.T
            sums = jnp.zeros((1, TILE), jnp.float32)
            for r in range(0, KB, 2 * STEP):
                re = value[r : r + STEP, :]
                im = value[r + STEP : r + 2 * STEP, :]
                right[1, r : r + 2 * STEP, cols] = jnp.concatenate([-im, re], axis=0)
                both = value[r : r + 2 * STEP, :].astype(jnp.float32)
                sums = sums + jnp.sum(both * both, axis=0, keepdims=True)
            if index == 0:
                power[:, cols] = sums
            else:
                power[:, cols] = power[:, cols] + sums
            return carry

        lax.fori_loop(0, S // TILE, block, 0)

        if g == 0:
            break

        def rows(i, carry):
            r = pl.ds(pl.multiple_of(i * TILE, TILE), TILE)

            def emit(cols, value):
                acc[r, cols] = value if index == 0 else acc[r, cols] + value

            products(i, j[r, :], right, emit)
            return carry

        lax.fori_loop(0, S // TILE, rows, 0)

    factor = 1.0 / jnp.sqrt(power[...] / FRAMES + 1e-06)
    power[...] = factor
    for b in range(0, S, 128):
        factor_col[b : b + 128, :] = jnp.broadcast_to(factor[:, b : b + 128], (128, 128)).T

    for g in range(CHUNKS):
        part = w.at[g, pl.ds(0, 127)]
        pltpu.make_async_copy(part, part, send_sem).wait()


def finish(acc, last, last_j, factor_row, factor_col, out, stage, sem):
    def arrival(slot):
        return pltpu.make_async_copy(stage.at[slot], out.at[0, pl.ds(0, TILE), :], sem.at[slot])

    def rows(i, slot, wait):
        pl.when(wait)(lambda: arrival(slot).wait())
        r = pl.ds(pl.multiple_of(i * TILE, TILE), TILE)
        scale = jnp.tile(factor_col[r, :], (1, TILE // 128)) * (1.0 / FRAMES)

        def emit(cols, value):
            stage[slot, :, cols] = (acc[r, cols] + value) * scale * factor_row[:, cols]

        products(i, last_j[r, :], last, emit)
        pltpu.make_async_copy(stage.at[slot], out.at[0, r, :], sem.at[slot]).start()

    def some(p, carry):
        for slot in range(SLOTS):
            rows(SLOTS * p + slot, slot, p > 0)
        return carry

    lax.fori_loop(0, S // TILE // SLOTS, some, 0)
    for slot in range(SLOTS):
        arrival(slot).wait()


def body(voltages):
    vmem = pl.BlockSpec(memory_space=pltpu.VMEM)
    hbm = pl.BlockSpec(memory_space=pl.ANY)
    dma = pltpu.SemaphoreType.DMA
    parts = pl.pallas_call(
        exchange,
        out_shape=[
            pltpu.VMEM((S, S), jnp.float32),
            pltpu.VMEM((2, KB, S), jnp.bfloat16),
            pltpu.VMEM((S, KB), jnp.bfloat16),
            pltpu.VMEM((1, S), jnp.float32),
            pltpu.VMEM((S, 128), jnp.float32),
        ],
        in_specs=[hbm],
        out_specs=[vmem] * 5,
        scratch_shapes=[
            pltpu.VMEM((ROWS, (FR_DEV + TAPS - 1) * L), jnp.bfloat16),
            pltpu.VMEM((TAPS, L), jnp.float32),
            pltpu.VMEM((TAPS, L), jnp.float32),
            pltpu.VMEM((2 * CHAN, L), jnp.bfloat16),
            pltpu.VMEM((2, 2 * ROWS, L), jnp.bfloat16),
            pltpu.VMEM((STEP * 2 * CHAN, ROWS), jnp.float32),
            pltpu.VMEM((CHUNKS, CHAN, 2 * STEP, ROWS), jnp.bfloat16),
            pltpu.VMEM((CHUNKS - 1, 2, KB, S), jnp.bfloat16),
            pltpu.VMEM((S, KB), jnp.bfloat16),
            dma((3,)),
            dma((2,)),
            dma((2,)),
            dma,
            dma((CHUNKS,)),
        ],
        compiler_params=pltpu.CompilerParams(
            collective_id=0, has_side_effects=True, vmem_limit_bytes=40 << 20
        ),
        name="exchange",
    )(voltages)
    return pl.pallas_call(
        finish,
        out_shape=jax.ShapeDtypeStruct((1, S, S), jnp.float32),
        in_specs=[vmem] * 5,
        out_specs=hbm,
        scratch_shapes=[pltpu.VMEM((SLOTS, TILE, S), jnp.float32), dma((SLOTS,))],
        compiler_params=pltpu.CompilerParams(vmem_limit_bytes=10 << 20),
        name="finish",
    )(*parts)


def solution(mesh):
    return jax.shard_map(
        body,
        mesh=mesh,
        in_specs=(P("wide", "narrow"),),
        out_specs=P(("wide", "narrow"), None, None),
        check_vma=False,
    )
```

```python
import functools
import math

import jax
import jax.numpy as jnp
from jax import lax
from jax.experimental import pallas as pl
from jax.experimental.pallas import tpu as pltpu
from jax.sharding import PartitionSpec as P

S = 2048
L = 512
TAPS = 4
CHAN = 128
FRAMES = 512
WIDE = 16
NARROW = 8
ROWS = S // WIDE
FR_DEV = FRAMES // NARROW
STEP = 16
CHUNKS = FR_DEV // STEP
ORDER = (1, 2, 3, 0)
KB = 2 * STEP * NARROW
TILE = 256
SLOTS = 4
MESH = pl.DeviceIdType.MESH


def channel_table():
    index = lax.broadcasted_iota(jnp.int32, (CHAN, L), 1)
    channel = lax.broadcasted_iota(jnp.int32, (CHAN, L), 0)
    angle = (index * channel % L).astype(jnp.float32) * (2.0 * math.pi / L)
    return jnp.concatenate([jnp.cos(angle), -jnp.sin(angle)], axis=0).astype(jnp.bfloat16)


def taper_table():
    tap = lax.broadcasted_iota(jnp.int32, (TAPS, L), 0)
    place = (tap * L + lax.broadcasted_iota(jnp.int32, (TAPS, L), 1)).astype(jnp.float32)
    offset = (place - TAPS * L / 2.0 + 0.5) * (math.pi / L)
    window = 0.5 - 0.5 * jnp.cos(2.0 * math.pi * (place + 0.5) / (TAPS * L))
    return jnp.sin(offset) / offset * window


def filtered(xv, filt, slot, half, base, weights, taps=TAPS):
    for r in range(0, ROWS, 16):
        total = None
        for tap in range(taps):
            part = xv[r : r + 16, pl.ds(pl.multiple_of(base + tap * L, L), L)]
            term = part.astype(jnp.float32) * weights[tap : tap + 1, :]
            total = term if total is None else total + term
        filt[slot, half * ROWS + r : half * ROWS + r + 16, :] = total.astype(jnp.bfloat16)


def transformed(table, filt, slot):
    return lax.dot_general(
        table[...], filt[slot], (((1,), (1,)), ((), ())), preferred_element_type=jnp.float32
    )


def make_chunk(g, xv, taper, taper_edge, table, filt, spec, w, complete):
    def group(p, carry):
        for slot in range(2):
            for half in range(2):
                f = g * STEP + 4 * p + 2 * slot + half
                filtered(xv, filt, slot, half, jnp.maximum(f - 1, 0) * L, taper)
            if g == 0 and slot == 0:

                @pl.when(p == 0)
                def _():
                    filtered(xv, filt, 0, 0, (FR_DEV - 1) * L, taper_edge)

            out = transformed(table, filt, slot)
            row = pl.multiple_of((4 * p + 2 * slot) * (2 * CHAN), 2 * 2 * CHAN)
            spec[pl.ds(row, 2 * CHAN), :] = out[:, :ROWS]
            spec[pl.ds(row + 2 * CHAN, 2 * CHAN), :] = out[:, ROWS:]
        return carry

    lax.fori_loop(0, STEP // 4, group, 0)
    if g == 0:
        complete()

    def turn(b, carry):
        for c in range(8):
            re = spec[pl.ds(8 * b + c, STEP, stride=2 * CHAN), :]
            im = spec[pl.ds(8 * b + c + CHAN, STEP, stride=2 * CHAN), :]
            w[8 * b + c] = jnp.concatenate([re, im], axis=0).astype(jnp.bfloat16)
        return carry

    lax.fori_loop(0, CHAN // 8, turn, 0)


def products(i, left, right, emit):
    def dot(kind, cols):
        return jnp.dot(left, right[kind, :, cols], preferred_element_type=jnp.float32)

    def columns(c):
        return pl.ds(pl.multiple_of(c * TILE, TILE), TILE)

    for t in range(1, S // TILE):
        c = (i + t) % (S // TILE)
        emit(columns(c), dot(jnp.where(c > i, 1, 0), columns(c)))
    row = lax.broadcasted_iota(jnp.int32, (TILE, TILE), 0)
    col = lax.broadcasted_iota(jnp.int32, (TILE, TILE), 1)
    emit(columns(i), jnp.where(row >= col, dot(0, columns(i)), dot(1, columns(i))))


def exchange(
    x_hbm, acc, last, last_j, power, factor_col,
    xv, taper, taper_edge, table, ahead_out, ahead_in, filt, spec, w, kt, j, load_sem, edge_send, edge_recv, send_sem, recv_sem,
):
    wide = lax.axis_index("wide")
    narrow = lax.axis_index("narrow")
    x, y, z, core = wide // 4, (wide // 2) % 2 * 2 + narrow // 4, narrow % 4, wide % 2
    mine = wide * NARROW + narrow

    def partners(q):
        for step in range(4):
            dy = (q % 4 + step) % 4
            px = (x + step) % 4
            py = (y + dy) % 4
            pz = (z + q // 4 + dy + step) % 4
            for flip in range(2):
                pc = (core + flip) % 2
                yield step == 0 and flip == 0, (px * 4 + py // 2 * 2 + pc, py % 2 * 4 + pz)

    def everyone(q, visit):
        for own, device in partners(q):
            if own:
                pl.when(q > 0)(functools.partial(visit, device))
            else:
                visit(device)

    barrier = pltpu.get_barrier_semaphore()

    def greet(q, carry):
        def signal(device):
            pl.semaphore_signal(barrier, inc=1, device_id=device, device_id_type=MESH)

        everyone(q, signal)
        return carry

    lax.fori_loop(0, 16, greet, 0)

    first = ORDER[0]
    pieces = [
        (FR_DEV - 2, FR_DEV),
        (first * STEP - 3, first * STEP + STEP),
        (first * STEP + STEP, FR_DEV - 2),
        (0, first * STEP - 3),
    ]
    loads = [
        pltpu.make_async_copy(
            x_hbm.at[:, begin * L : end * L], xv.at[:, (begin + 2) * L : (end + 2) * L], load_sem.at[index]
        )
        for index, (begin, end) in enumerate(pieces)
    ]
    for copy in loads:
        copy.start()
    xv[:, : 2 * L] = jnp.zeros((ROWS, 2 * L), jnp.bfloat16)
    taper[...] = taper_table()
    table[...] = channel_table()
    taper_edge[...] = taper[...] * jnp.where(
        (narrow == NARROW - 1) & (lax.broadcasted_iota(jnp.int32, (TAPS, L), 0) < TAPS - 1), 0.0, 1.0
    )

    ahead = pltpu.make_async_remote_copy(
        ahead_out,
        ahead_in,
        edge_send.at[0],
        edge_recv.at[0],
        device_id=(wide, (narrow + 1) % NARROW),
        device_id_type=MESH,
    )
    back = pltpu.make_async_remote_copy(
        x_hbm.at[:, :L],
        xv.at[:, (FR_DEV + 2) * L :],
        edge_send.at[1],
        edge_recv.at[1],
        device_id=(wide, (narrow + NARROW - 1) % NARROW),
        device_id_type=MESH,
    )

    def landing(g):
        return kt.at[g - 1, 0] if g > 0 else last.at[0]

    def send(g):
        row = pl.multiple_of(narrow * (2 * STEP), 2 * STEP)
        col = pl.multiple_of(wide * ROWS, ROWS)
        dst = landing(g).at[pl.ds(row, 2 * STEP), pl.ds(col, ROWS)]

        def one(q, carry):
            def start(device):
                pltpu.make_async_remote_copy(
                    w.at[g, device[0] * NARROW + device[1]],
                    dst,
                    send_sem,
                    recv_sem.at[g],
                    device_id=device,
                    device_id_type=MESH,
                ).start()

            everyone(q, start)
            return carry

        lax.fori_loop(0, 16, one, 0)
        pltpu.make_async_copy(w.at[g, mine], dst, recv_sem.at[g]).start()

    loads[0].wait()
    filtered(xv, filt, 0, 0, FR_DEV * L, taper, 2)
    filtered(xv, filt, 0, 1, (FR_DEV + 1) * L, taper, 1)
    out = transformed(table, filt, 0).astype(jnp.bfloat16)
    ahead_out[: 2 * CHAN, :] = out[:, :ROWS]
    ahead_out[2 * CHAN :, :] = out[:, ROWS:]

    def complete():
        @pl.when(narrow > 0)
        def _():
            rows = slice(2 * CHAN, 3 * 2 * CHAN)
            spec[rows, :] = spec[rows, :] + ahead_in[...].astype(jnp.float32)

    pl.semaphore_wait(barrier, 127)
    ahead.start()
    back.start()
    for index, g in enumerate(ORDER):
        if index + 1 < len(loads):
            loads[index + 1].wait()
        if g == 0:
            ahead.wait()
            back.wait()
        make_chunk(g, xv, taper, taper_edge, table, filt, spec, w.at[g], complete)
        send(g)

    for index, g in enumerate(ORDER):
        right = last if g == 0 else kt.at[g - 1]
        left = last_j if g == 0 else j
        pltpu.make_async_copy(right.at[0], right.at[0], recv_sem.at[g]).wait()

        def block(b, carry):
            cols = pl.ds(pl.multiple_of(b * TILE, TILE), TILE)
            value = right[0, :, cols]
            left[cols, :] = value.T
            sums = jnp.zeros((1, TILE), jnp.float32)
            for r in range(0, KB, 2 * STEP):
                re = value[r : r + STEP, :]
                im = value[r + STEP : r + 2 * STEP, :]
                right[1, r : r + 2 * STEP, cols] = jnp.concatenate([-im, re], axis=0)
                both = value[r : r + 2 * STEP, :].astype(jnp.float32)
                sums = sums + jnp.sum(both * both, axis=0, keepdims=True)
            if index == 0:
                power[:, cols] = sums
            else:
                power[:, cols] = power[:, cols] + sums
            return carry

        lax.fori_loop(0, S // TILE, block, 0)

        if g == 0:
            break

        def rows(i, carry):
            r = pl.ds(pl.multiple_of(i * TILE, TILE), TILE)

            def emit(cols, value):
                acc[r, cols] = value if index == 0 else acc[r, cols] + value

            products(i, j[r, :], right, emit)
            return carry

        lax.fori_loop(0, S // TILE, rows, 0)

    factor = 1.0 / jnp.sqrt(power[...] / FRAMES + 1e-06)
    power[...] = factor
    for b in range(0, S, 128):
        factor_col[b : b + 128, :] = jnp.broadcast_to(factor[:, b : b + 128], (128, 128)).T

    for g in range(CHUNKS):
        part = w.at[g, pl.ds(0, 127)]
        pltpu.make_async_copy(part, part, send_sem).wait()


def finish(acc, last, last_j, factor_row, factor_col, out, stage, sem):
    def arrival(slot):
        return pltpu.make_async_copy(stage.at[slot], out.at[0, pl.ds(0, TILE), :], sem.at[slot])

    def rows(i, slot, wait):
        pl.when(wait)(lambda: arrival(slot).wait())
        r = pl.ds(pl.multiple_of(i * TILE, TILE), TILE)
        scale = jnp.tile(factor_col[r, :], (1, TILE // 128)) * (1.0 / FRAMES)

        def emit(cols, value):
            stage[slot, :, cols] = (acc[r, cols] + value) * scale * factor_row[:, cols]

        products(i, last_j[r, :], last, emit)
        pltpu.make_async_copy(stage.at[slot], out.at[0, r, :], sem.at[slot]).start()

    def some(p, carry):
        for slot in range(SLOTS):
            rows(SLOTS * p + slot, slot, p > 0)
        return carry

    lax.fori_loop(0, S // TILE // SLOTS, some, 0)
    for slot in range(SLOTS):
        arrival(slot).wait()


def body(voltages):
    vmem = pl.BlockSpec(memory_space=pltpu.VMEM)
    hbm = pl.BlockSpec(memory_space=pl.ANY)
    dma = pltpu.SemaphoreType.DMA
    parts = pl.pallas_call(
        exchange,
        out_shape=[
            pltpu.VMEM((S, S), jnp.float32),
            pltpu.VMEM((2, KB, S), jnp.bfloat16),
            pltpu.VMEM((S, KB), jnp.bfloat16),
            pltpu.VMEM((1, S), jnp.float32),
            pltpu.VMEM((S, 128), jnp.float32),
        ],
        in_specs=[hbm],
        out_specs=[vmem] * 5,
        scratch_shapes=[
            pltpu.VMEM((ROWS, (FR_DEV + TAPS - 1) * L), jnp.bfloat16),
            pltpu.VMEM((TAPS, L), jnp.float32),
            pltpu.VMEM((TAPS, L), jnp.float32),
            pltpu.VMEM((2 * CHAN, L), jnp.bfloat16),
            pltpu.VMEM((2 * 2 * CHAN, ROWS), jnp.bfloat16),
            pltpu.VMEM((2 * 2 * CHAN, ROWS), jnp.bfloat16),
            pltpu.VMEM((2, 2 * ROWS, L), jnp.bfloat16),
            pltpu.VMEM((STEP * 2 * CHAN, ROWS), jnp.float32),
            pltpu.VMEM((CHUNKS, CHAN, 2 * STEP, ROWS), jnp.bfloat16),
            pltpu.VMEM((CHUNKS - 1, 2, KB, S), jnp.bfloat16),
            pltpu.VMEM((S, KB), jnp.bfloat16),
            dma((4,)),
            dma((2,)),
            dma((2,)),
            dma,
            dma((CHUNKS,)),
        ],
        compiler_params=pltpu.CompilerParams(
            collective_id=0, has_side_effects=True, vmem_limit_bytes=40 << 20
        ),
        name="exchange",
    )(voltages)
    return pl.pallas_call(
        finish,
        out_shape=jax.ShapeDtypeStruct((1, S, S), jnp.float32),
        in_specs=[vmem] * 5,
        out_specs=hbm,
        scratch_shapes=[pltpu.VMEM((SLOTS, TILE, S), jnp.float32), dma((SLOTS,))],
        compiler_params=pltpu.CompilerParams(vmem_limit_bytes=10 << 20),
        name="finish",
    )(*parts)


def solution(mesh):
    return jax.shard_map(
        body,
        mesh=mesh,
        in_specs=(P("wide", "narrow"),),
        out_specs=P(("wide", "narrow"), None, None),
        check_vma=False,
    )
```

```python
import functools
import math

import jax
import jax.numpy as jnp
from jax import lax
from jax.experimental import pallas as pl
from jax.experimental.pallas import tpu as pltpu
from jax.sharding import PartitionSpec as P

S = 2048
L = 512
TAPS = 4
CHAN = 128
FRAMES = 512
WIDE = 16
NARROW = 8
ROWS = S // WIDE
FR_DEV = FRAMES // NARROW
STEP = 16
CHUNKS = FR_DEV // STEP
ORDER = (1, 2, 3, 0)
KB = 2 * STEP * NARROW
TILE = 256
SLOTS = 4
MESH = pl.DeviceIdType.MESH


def channel_table():
    index = lax.broadcasted_iota(jnp.int32, (CHAN, L), 1)
    channel = lax.broadcasted_iota(jnp.int32, (CHAN, L), 0)
    angle = (index * channel % L).astype(jnp.float32) * (2.0 * math.pi / L)
    return jnp.concatenate([jnp.cos(angle), -jnp.sin(angle)], axis=0).astype(jnp.bfloat16)


def taper_table():
    tap = lax.broadcasted_iota(jnp.int32, (TAPS, L), 0)
    place = (tap * L + lax.broadcasted_iota(jnp.int32, (TAPS, L), 1)).astype(jnp.float32)
    offset = (place - TAPS * L / 2.0 + 0.5) * (math.pi / L)
    window = 0.5 - 0.5 * jnp.cos(2.0 * math.pi * (place + 0.5) / (TAPS * L))
    return jnp.sin(offset) / offset * window


def filtered(xv, filt, slot, half, base, weights, taps=TAPS):
    for r in range(0, ROWS, 16):
        total = None
        for tap in range(taps):
            part = xv[r : r + 16, pl.ds(pl.multiple_of(base + tap * L, L), L)]
            term = part.astype(jnp.float32) * weights[tap : tap + 1, :]
            total = term if total is None else total + term
        filt[slot, half * ROWS + r : half * ROWS + r + 16, :] = total.astype(jnp.bfloat16)


def transformed(table, filt, slot):
    return lax.dot_general(
        table[...], filt[slot], (((1,), (1,)), ((), ())), preferred_element_type=jnp.float32
    )


def make_chunk(g, xv, taper, taper_edge, table, filt, spec, w, complete):
    def group(p, carry):
        for slot in range(2):
            for half in range(2):
                f = g * STEP + 4 * p + 2 * slot + half
                filtered(xv, filt, slot, half, jnp.maximum(f - 1, 0) * L, taper)
            if g == 0 and slot == 0:

                @pl.when(p == 0)
                def _():
                    filtered(xv, filt, 0, 0, (FR_DEV - 1) * L, taper_edge)

            out = transformed(table, filt, slot)
            row = pl.multiple_of((4 * p + 2 * slot) * (2 * CHAN), 2 * 2 * CHAN)
            spec[pl.ds(row, 2 * CHAN), :] = out[:, :ROWS]
            spec[pl.ds(row + 2 * CHAN, 2 * CHAN), :] = out[:, ROWS:]
        return carry

    lax.fori_loop(0, STEP // 4, group, 0)
    if g == 0:
        complete()

    def turn(b, carry):
        for c in range(8):
            re = spec[pl.ds(8 * b + c, STEP, stride=2 * CHAN), :]
            im = spec[pl.ds(8 * b + c + CHAN, STEP, stride=2 * CHAN), :]
            w[8 * b + c] = jnp.concatenate([re, im], axis=0).astype(jnp.bfloat16)
        return carry

    lax.fori_loop(0, CHAN // 8, turn, 0)


def products(i, left, right, emit):
    def dot(kind, cols):
        return jnp.dot(left, right[kind, :, cols], preferred_element_type=jnp.float32)

    def columns(c):
        return pl.ds(pl.multiple_of(c * TILE, TILE), TILE)

    for t in range(1, S // TILE):
        c = (i + t) % (S // TILE)
        emit(columns(c), dot(jnp.where(c > i, 1, 0), columns(c)))
    row = lax.broadcasted_iota(jnp.int32, (TILE, TILE), 0)
    col = lax.broadcasted_iota(jnp.int32, (TILE, TILE), 1)
    emit(columns(i), jnp.where(row >= col, dot(0, columns(i)), dot(1, columns(i))))


def exchange(
    x_hbm, acc, last, last_j, power, factor_col,
    xv, taper, taper_edge, table, ahead_out, ahead_in, filt, spec, w, kt, j, load_sem, edge_send, edge_recv, send_sem, recv_sem,
):
    wide = lax.axis_index("wide")
    narrow = lax.axis_index("narrow")
    x, y, z, core = wide // 4, (wide // 2) % 2 * 2 + narrow // 4, narrow % 4, wide % 2
    mine = wide * NARROW + narrow

    def partners(q):
        for step in range(4):
            dy = (q % 4 + step) % 4
            px = (x + step) % 4
            py = (y + dy) % 4
            pz = (z + q // 4 + dy + step) % 4
            for flip in range(2):
                pc = (core + flip) % 2
                yield step == 0 and flip == 0, (px * 4 + py // 2 * 2 + pc, py % 2 * 4 + pz)

    def everyone(q, visit):
        for own, device in partners(q):
            if own:
                pl.when(q > 0)(functools.partial(visit, device))
            else:
                visit(device)

    barrier = pltpu.get_barrier_semaphore()

    def greet(q, carry):
        def signal(device):
            pl.semaphore_signal(barrier, inc=1, device_id=device, device_id_type=MESH)

        everyone(q, signal)
        return carry

    lax.fori_loop(0, 16, greet, 0)

    first = ORDER[0]
    pieces = [
        (FR_DEV - 2, FR_DEV),
        (first * STEP - 3, first * STEP + STEP),
        (first * STEP + STEP, FR_DEV - 2),
        (0, first * STEP - 3),
    ]
    loads = [
        pltpu.make_async_copy(
            x_hbm.at[:, begin * L : end * L], xv.at[:, (begin + 2) * L : (end + 2) * L], load_sem.at[index]
        )
        for index, (begin, end) in enumerate(pieces)
    ]
    for copy in loads:
        copy.start()
    xv[:, : 2 * L] = jnp.zeros((ROWS, 2 * L), jnp.bfloat16)
    taper[...] = taper_table()
    table[...] = channel_table()
    taper_edge[...] = taper[...] * jnp.where(
        (narrow == NARROW - 1) & (lax.broadcasted_iota(jnp.int32, (TAPS, L), 0) < TAPS - 1), 0.0, 1.0
    )

    ahead = pltpu.make_async_remote_copy(
        ahead_out,
        ahead_in,
        edge_send.at[0],
        edge_recv.at[0],
        device_id=(wide, (narrow + 1) % NARROW),
        device_id_type=MESH,
    )
    back = pltpu.make_async_remote_copy(
        x_hbm.at[:, :L],
        xv.at[:, (FR_DEV + 2) * L :],
        edge_send.at[1],
        edge_recv.at[1],
        device_id=(wide, (narrow + NARROW - 1) % NARROW),
        device_id_type=MESH,
    )

    def landing(g):
        return kt.at[g - 1, 0] if g > 0 else last.at[0]

    def send(g):
        row = pl.multiple_of(narrow * (2 * STEP), 2 * STEP)
        col = pl.multiple_of(wide * ROWS, ROWS)
        dst = landing(g).at[pl.ds(row, 2 * STEP), pl.ds(col, ROWS)]

        def one(q, carry):
            def start(device):
                pltpu.make_async_remote_copy(
                    w.at[g, device[0] * NARROW + device[1]],
                    dst,
                    send_sem,
                    recv_sem.at[g],
                    device_id=device,
                    device_id_type=MESH,
                ).start()

            everyone(q, start)
            return carry

        lax.fori_loop(0, 16, one, 0)
        pltpu.make_async_copy(w.at[g, mine], dst, recv_sem.at[g]).start()

    loads[0].wait()
    filtered(xv, filt, 0, 0, FR_DEV * L, taper, 2)
    filtered(xv, filt, 0, 1, (FR_DEV + 1) * L, taper, 1)
    out = transformed(table, filt, 0).astype(jnp.bfloat16)
    ahead_out[: 2 * CHAN, :] = out[:, :ROWS]
    ahead_out[2 * CHAN :, :] = out[:, ROWS:]

    def complete():
        @pl.when(narrow > 0)
        def _():
            rows = slice(2 * CHAN, 3 * 2 * CHAN)
            spec[rows, :] = spec[rows, :] + ahead_in[...].astype(jnp.float32)

    for index, g in enumerate(ORDER):
        if index + 1 < len(loads):
            loads[index + 1].wait()
        if g == 0:
            ahead.wait()
            back.wait()
        make_chunk(g, xv, taper, taper_edge, table, filt, spec, w.at[g], complete)
        if index == 0:
            pl.semaphore_wait(barrier, 127)
            ahead.start()
            back.start()
        send(g)

    for index, g in enumerate(ORDER):
        right = last if g == 0 else kt.at[g - 1]
        left = last_j if g == 0 else j
        pltpu.make_async_copy(right.at[0], right.at[0], recv_sem.at[g]).wait()

        def block(b, carry):
            cols = pl.ds(pl.multiple_of(b * TILE, TILE), TILE)
            value = right[0, :, cols]
            left[cols, :] = value.T
            sums = jnp.zeros((1, TILE), jnp.float32)
            for r in range(0, KB, 2 * STEP):
                re = value[r : r + STEP, :]
                im = value[r + STEP : r + 2 * STEP, :]
                right[1, r : r + 2 * STEP, cols] = jnp.concatenate([-im, re], axis=0)
                both = value[r : r + 2 * STEP, :].astype(jnp.float32)
                sums = sums + jnp.sum(both * both, axis=0, keepdims=True)
            if index == 0:
                power[:, cols] = sums
            else:
                power[:, cols] = power[:, cols] + sums
            return carry

        lax.fori_loop(0, S // TILE, block, 0)

        if g == 0:
            break

        def rows(i, carry):
            r = pl.ds(pl.multiple_of(i * TILE, TILE), TILE)

            def emit(cols, value):
                acc[r, cols] = value if index == 0 else acc[r, cols] + value

            products(i, j[r, :], right, emit)
            return carry

        lax.fori_loop(0, S // TILE, rows, 0)

    factor = 1.0 / jnp.sqrt(power[...] / FRAMES + 1e-06)
    power[...] = factor
    for b in range(0, S, 128):
        factor_col[b : b + 128, :] = jnp.broadcast_to(factor[:, b : b + 128], (128, 128)).T

    for g in range(CHUNKS):
        part = w.at[g, pl.ds(0, 127)]
        pltpu.make_async_copy(part, part, send_sem).wait()


def finish(acc, last, last_j, factor_row, factor_col, out, stage, sem):
    def arrival(slot):
        return pltpu.make_async_copy(stage.at[slot], out.at[0, pl.ds(0, TILE), :], sem.at[slot])

    def rows(i, slot, wait):
        pl.when(wait)(lambda: arrival(slot).wait())
        r = pl.ds(pl.multiple_of(i * TILE, TILE), TILE)
        scale = jnp.tile(factor_col[r, :], (1, TILE // 128)) * (1.0 / FRAMES)

        def emit(cols, value):
            stage[slot, :, cols] = (acc[r, cols] + value) * scale * factor_row[:, cols]

        products(i, last_j[r, :], last, emit)
        pltpu.make_async_copy(stage.at[slot], out.at[0, r, :], sem.at[slot]).start()

    def some(p, carry):
        for slot in range(SLOTS):
            rows(SLOTS * p + slot, slot, p > 0)
        return carry

    lax.fori_loop(0, S // TILE // SLOTS, some, 0)
    for slot in range(SLOTS):
        arrival(slot).wait()


def body(voltages):
    vmem = pl.BlockSpec(memory_space=pltpu.VMEM)
    hbm = pl.BlockSpec(memory_space=pl.ANY)
    dma = pltpu.SemaphoreType.DMA
    parts = pl.pallas_call(
        exchange,
        out_shape=[
            pltpu.VMEM((S, S), jnp.float32),
            pltpu.VMEM((2, KB, S), jnp.bfloat16),
            pltpu.VMEM((S, KB), jnp.bfloat16),
            pltpu.VMEM((1, S), jnp.float32),
            pltpu.VMEM((S, 128), jnp.float32),
        ],
        in_specs=[hbm],
        out_specs=[vmem] * 5,
        scratch_shapes=[
            pltpu.VMEM((ROWS, (FR_DEV + TAPS - 1) * L), jnp.bfloat16),
            pltpu.VMEM((TAPS, L), jnp.float32),
            pltpu.VMEM((TAPS, L), jnp.float32),
            pltpu.VMEM((2 * CHAN, L), jnp.bfloat16),
            pltpu.VMEM((2 * 2 * CHAN, ROWS), jnp.bfloat16),
            pltpu.VMEM((2 * 2 * CHAN, ROWS), jnp.bfloat16),
            pltpu.VMEM((2, 2 * ROWS, L), jnp.bfloat16),
            pltpu.VMEM((STEP * 2 * CHAN, ROWS), jnp.float32),
            pltpu.VMEM((CHUNKS, CHAN, 2 * STEP, ROWS), jnp.bfloat16),
            pltpu.VMEM((CHUNKS - 1, 2, KB, S), jnp.bfloat16),
            pltpu.VMEM((S, KB), jnp.bfloat16),
            dma((4,)),
            dma((2,)),
            dma((2,)),
            dma,
            dma((CHUNKS,)),
        ],
        compiler_params=pltpu.CompilerParams(
            collective_id=0, has_side_effects=True, vmem_limit_bytes=40 << 20
        ),
        name="exchange",
    )(voltages)
    return pl.pallas_call(
        finish,
        out_shape=jax.ShapeDtypeStruct((1, S, S), jnp.float32),
        in_specs=[vmem] * 5,
        out_specs=hbm,
        scratch_shapes=[pltpu.VMEM((SLOTS, TILE, S), jnp.float32), dma((SLOTS,))],
        compiler_params=pltpu.CompilerParams(vmem_limit_bytes=10 << 20),
        name="finish",
    )(*parts)


def solution(mesh):
    return jax.shard_map(
        body,
        mesh=mesh,
        in_specs=(P("wide", "narrow"),),
        out_specs=P(("wide", "narrow"), None, None),
        check_vma=False,
    )
```
